32 devices in a mesh: groups: 2 (over x), dp: 8 (over z, y), owner: 2 (over core).
Axes of the slice: x: 2, y: 2, z: 4, core: 2. Of those that a mesh axis runs over, the one named last changes fastest.
Arguments:
- inputs: bfloat16 [2, 8192, 1408], P('owner', ('groups', 'dp')), parts along dimension 1, may hold values from -6 to 6
- grad_weight: bfloat16 [2816, 1408], P('groups'), parts along dimension 0, may hold values from -6 to 6
- counts: int32 [16], P('groups'), parts along dimension 0, may hold values from 128 to 512
- owners: int32 [4], P('groups'), parts along dimension 0, may hold values from 0 to 7
Outputs:
- kept_inverse: bfloat16 [16, 2, 1408, 1408], P(('groups', 'dp'), 'owner'), parts along dimension 0
- precond: bfloat16 [2816, 1408], P(('groups', 'dp', 'owner')), parts along dimension 0
The draws below stay inside these ranges and needn't reach their ends.
There are 2 independent parts, one for each index of `groups`. The reference program is written for one: setup_inputs(seed, part) draws one part's arguments, and reference() takes and returns one part's arrays. A program takes and returns all parts, laid end to end along the dimension named above; each array names one. Nothing has to cross between parts.
Inputs may be any that keep to these rules, and one draw needn't show every extreme that they name: `counts`: live tokens come first in each shard's slots. Core k of chip owners[k] owns factor k; both factors may have the same chip.
All inputs are finite; a program needn't handle non-finite values.
Results may differ from the reference program's by a relative error of at most 0.0065.
Values may be sent and summed in bfloat16 or wider, within the bound.
No kernel may reach another device: no remote copies, remote signals or barrier semaphores. Data moves between devices by JAX's collectives and lax.ppermute only.
A program may use at most 192 MiB of HBM per device.

```python
import jax
import jax.numpy as jnp
from jax import lax

D = 1408
TOK_DEV = 512
FACTORS = 2
TOKENS = 4096
N_DP = 8


def place_ends(array, stream_key, smallest, high):
    longest = array.shape.index(max(array.shape))
    spots = []
    for shift in (0, 1):
        where = [jax.random.randint(jax.random.fold_in(stream_key, axis), (), 0, length) for axis, length in enumerate(array.shape)]
        where[longest] = (where[longest] + shift) % array.shape[longest]
        spots.append(tuple(where))
    return array.at[spots[0]].set(smallest).at[spots[1]].set(high)


def with_spikes(array, key, source, target, blocks, factor):
    def block_of(dim):
        return (jnp.arange(array.shape[dim]) // (array.shape[dim] // blocks)).reshape((-1,) + (1,) * (array.ndim - 1 - dim))

    first = jax.random.permutation(key, blocks)[block_of(target)]
    far = (block_of(target) + blocks // 2) % blocks
    return jnp.where((block_of(source) == first) | (block_of(source) == far), factor * array, array)


def shard_levels(rng, extent, split, low, high):
    def one(axis_at, parts):
        draws = jax.random.uniform(jax.random.fold_in(jax.random.fold_in(rng, 6), axis_at), (parts,), jnp.float32, low / len(split), high / len(split))
        return jnp.repeat(jnp.exp(draws), extent[axis_at] // parts).reshape((-1,) + (1,) * (len(extent) - axis_at - 1))

    gain = one(*split[0])
    for cut in split[1:]:
        gain = gain * one(*cut)
    return gain


def centred(own_key, extent, deviation, bound, shards=(), kind=jnp.bfloat16):
    entries = deviation * jax.random.normal(own_key, extent, jnp.float32)
    if shards:
        entries = entries * shard_levels(own_key, extent, shards, -0.22, 0.18)
    return jnp.clip(entries, -bound, bound).astype(kind)


def heavy_noise(own_key, extent, scale, most, split, heavy, held_as=jnp.bfloat16):
    entries = scale * jax.random.normal(own_key, extent, jnp.float32)
    if split:
        entries = entries * shard_levels(own_key, extent, split, -0.22, 0.18)
    return jnp.clip(with_spikes(entries, jax.random.fold_in(own_key, 3), *heavy), -most, most).astype(held_as)


def setup_inputs(seed: int = 0, part: int = 0) -> dict:
    seeds = jax.random.split(jax.random.key(seed), 5)
    own_keys = jax.random.split(jax.random.fold_in(seeds[4], part), 5)
    inputs = heavy_noise(own_keys[0], (FACTORS, TOKENS, D), 1.0, 6.0, ((0, 2), (1, 8)), (1, 2, 8, 2.0))
    grad_weight = centred(own_keys[1], (D, D), 1.0, 6.0)
    counts = place_ends(jax.random.randint(own_keys[2], (N_DP,), TOK_DEV // 4, TOK_DEV + 1), jax.random.fold_in(own_keys[2], 1), TOK_DEV // 4, TOK_DEV).astype(jnp.int32)
    owners = jax.random.randint(own_keys[3], (FACTORS,), 0, N_DP).astype(jnp.int32)
    return dict(inputs=inputs, grad_weight=grad_weight, counts=counts, owners=owners)


damping_term = 0.1

def chol_inverse(matrix):
    triangle = jnp.linalg.cholesky(matrix)
    identity = jnp.eye(matrix.shape[0], dtype=jnp.float32)
    return jax.scipy.linalg.cho_solve((triangle, True), identity)

def block_inverse(damped):
    half_width = damped.shape[0] // 2
    upper_left = damped[:half_width, :half_width]
    upper_right = damped[:half_width, half_width:]
    lower_right = damped[half_width:, half_width:]
    best = lax.Precision.HIGHEST
    left_inverse = chol_inverse(upper_left)
    weighted = jnp.dot(left_inverse, upper_right, precision=best)
    schur = lower_right - jnp.dot(upper_right.T, weighted, precision=best)
    schur_inverse = chol_inverse(schur)
    across = jnp.dot(weighted, schur_inverse, precision=best)
    top_left = left_inverse + jnp.dot(across, weighted.T, precision=best)
    top_row = jnp.concatenate([top_left, -across], axis=1)
    bottom_row = jnp.concatenate([-across.T, schur_inverse], axis=1)
    return jnp.concatenate([top_row, bottom_row], axis=0)

def reference(inputs, grad_weight, counts, owners):
    live_rows = (jnp.arange(TOK_DEV)[None, :] < counts[:, None]).reshape(-1)
    token_total = jnp.sum(counts).astype(jnp.float32)
    identity = jnp.eye(D, dtype=jnp.float32)
    contract = (((0,), (0,)), ((), ()))
    inverses = []
    for factor_kind in range(FACTORS):
        samples = inputs[factor_kind]
        masked = jnp.where(live_rows[:, None], samples, jnp.zeros_like(samples))
        summed = lax.dot_general(masked.astype(jnp.float32), samples.astype(jnp.float32), contract, preferred_element_type=jnp.float32)
        damped = summed / token_total + damping_term * identity
        inverses.append(block_inverse(damped).astype(jnp.bfloat16))
    stacked = jnp.stack(inverses)
    chosen = jnp.arange(N_DP)[:, None] == owners[None, :]
    kept_inverse = jnp.where(chosen[:, :, None, None], stacked[None], jnp.zeros((), jnp.bfloat16))
    left_product = jnp.dot(grad_weight.astype(jnp.float32), inverses[0].astype(jnp.float32), preferred_element_type=jnp.float32).astype(jnp.bfloat16)
    precond = jnp.dot(inverses[1].astype(jnp.float32), left_product.astype(jnp.float32), preferred_element_type=jnp.float32).astype(jnp.bfloat16)
    return (kept_inverse, precond)
```

```python
import functools

import jax
import jax.numpy as jnp
from jax import lax
from jax.experimental import pallas as pl
from jax.experimental.pallas import tpu as pltpu
from jax.sharding import PartitionSpec as P

damping_term = 0.1
TILE = 128
f32 = jnp.float32
bf16 = jnp.bfloat16


def split3(x):
    a = x.astype(bf16)
    r = x - a.astype(f32)
    b = r.astype(bf16)
    c = (r - b.astype(f32)).astype(bf16)
    return a, b, c


def left_parts(x):
    a, b, c = split3(x)
    return jnp.concatenate([a, a, b, a, b, c], axis=1)


def right_parts(x):
    a, b, c = split3(x)
    return jnp.concatenate([a, b, a, c, b, a], axis=0)


def mm(a, b):
    return jnp.dot(a, b, preferred_element_type=f32)


def all_rows(x, p):
    return jnp.broadcast_to(x[p : p + 1, :], x.shape)


def tree_sum(xs):
    while len(xs) > 1:
        xs = [xs[i] + xs[i + 1] if i + 1 < len(xs) else xs[i] for i in range(0, len(xs), 2)]
    return xs[0]


def sweep8(M, g):
    n = M.shape[0]
    p0 = 8 * g
    lane = lax.broadcasted_iota(jnp.int32, (8, n), 1)
    sub = lax.broadcasted_iota(jnp.int32, (8, n), 0)
    inside = (lane >= p0) & (lane < p0 + 8)
    R = M[p0 : p0 + 8, :]
    V = [jnp.broadcast_to(R[:, p0 + j : p0 + j + 1], (8, n)) for j in range(8)]
    for p in range(8):
        at = sub == p
        inv = 1.0 / all_rows(V[p], p)
        Vp = jnp.where(at, -1.0, V[p])
        V = [
            Vp * inv if j == p else jnp.where(at, 0.0, V[j]) - Vp * (all_rows(V[j], p) * inv)
            for j in range(8)
        ]
    Rq = jnp.where(inside, jnp.where(lane - p0 == sub, 1.0, 0.0), -R)
    W = tree_sum([V[r] * all_rows(Rq, r) for r in range(8)])
    Wb = [all_rows(W, r) for r in range(8)]
    out = []
    for i in range(n // 8):
        if i == g:
            out.append(W)
            continue
        Mi = M[8 * i : 8 * i + 8, :]
        t = [jnp.broadcast_to(Mi[:, p0 + r : p0 + r + 1], (8, n)) * Wb[r] for r in range(8)]
        out.append(jnp.where(inside, 0.0, Mi) - tree_sum(t))
    return jnp.concatenate(out, axis=0)


def sweep_tile(M):
    for g in range(M.shape[0] // 8):
        M = sweep8(M, g)
    return M


def factor_kernel(count_ref, x_ref, out_ref):
    rows, n = x_ref.shape
    x = x_ref[...]
    live = lax.broadcasted_iota(jnp.int32, (rows, n), 0) < count_ref[0]
    x = jnp.where(live, x, jnp.zeros_like(x))
    xt = x.T
    at = 0
    for i in range(n // TILE):
        row = mm(xt[i * TILE : (i + 1) * TILE, :], x[:, : (i + 1) * TILE])
        for j in range(i + 1):
            out_ref[at : at + TILE, :] = row[:, j * TILE : (j + 1) * TILE]
            at += TILE


def invert_kernel(scale_ref, keep_ref, tiles_ref, inv_ref, kept_ref, A, Cs, Ws, Wf, N):
    n = A.shape[0]
    blocks = n // TILE
    scale = scale_ref[0]
    eye = jnp.where(
        lax.broadcasted_iota(jnp.int32, (TILE, TILE), 0)
        == lax.broadcasted_iota(jnp.int32, (TILE, TILE), 1),
        damping_term,
        0.0,
    )
    at = 0
    for i in range(blocks):
        for j in range(i + 1):
            t = tiles_ref[at : at + TILE, :] * scale
            at += TILE
            if i == j:
                t = t + eye
            A[i * TILE : (i + 1) * TILE, j * TILE : (j + 1) * TILE] = t
            if i != j:
                A[j * TILE : (j + 1) * TILE, i * TILE : (i + 1) * TILE] = t.T
    N[...] = sweep_tile(A[:TILE, :TILE])
    wide = 2 * TILE

    def step(k, _):
        here = pl.ds(pl.multiple_of(k * TILE, TILE), TILE)
        later = pl.ds(pl.multiple_of(jnp.minimum(k + 1, blocks - 1) * TILE, TILE), TILE)
        D = N[...]
        Nl = left_parts(D)
        Nr = right_parts(D)
        for c in range(0, n, wide):
            w = min(wide, n - c)
            Wc = mm(Nl, right_parts(A[here, c : c + w]))
            Wf[:, c : c + w] = Wc
            Ws[:, c : c + w] = right_parts(Wc)
        for r in range(0, n, wide):
            h = min(wide, n - r)
            Cs[r : r + h, :] = left_parts(A[r : r + h, here])
        T = A[later, later] + mm(Cs[later, :], Ws[:, later])
        N[...] = sweep_tile(T)
        for c in range(0, n, wide):
            w = min(wide, n - c)
            A[:, c : c + w] = A[:, c : c + w] + mm(Cs[...], Ws[:, c : c + w])
        A[:, here] = -mm(Cs[...], Nr)
        A[here, :] = -Wf[...]
        A[here, here] = D
        return 0

    lax.fori_loop(0, blocks, step, 0)
    keep = keep_ref[0] != 0
    for i in range(blocks):
        rows = slice(i * TILE, (i + 1) * TILE)
        r = (-A[rows, :]).astype(bf16)
        inv_ref[rows, :] = r
        kept_ref[rows, :] = jnp.where(keep, r, jnp.zeros_like(r))


def vmem():
    return pl.BlockSpec(memory_space=pltpu.VMEM)


def smem():
    return pl.BlockSpec(memory_space=pltpu.SMEM)


def packed_factor(samples, count):
    n = samples.shape[1]
    blocks = n // TILE
    tiles = blocks * (blocks + 1) // 2
    return pl.pallas_call(
        factor_kernel,
        out_shape=jax.ShapeDtypeStruct((tiles * TILE, TILE), f32),
        in_specs=[smem(), vmem()],
        out_specs=vmem(),
        compiler_params=pltpu.CompilerParams(vmem_limit_bytes=48 << 20),
        name="factor_terms",
    )(count, samples)


def invert(tiles, scale, keep, n):
    return pl.pallas_call(
        invert_kernel,
        out_shape=[jax.ShapeDtypeStruct((n, n), bf16)] * 2,
        in_specs=[smem(), smem(), vmem()],
        out_specs=[vmem(), vmem()],
        scratch_shapes=[
            pltpu.VMEM((n, n), f32),
            pltpu.VMEM((n, 6 * TILE), bf16),
            pltpu.VMEM((6 * TILE, n), bf16),
            pltpu.VMEM((TILE, n), f32),
            pltpu.VMEM((TILE, TILE), f32),
        ],
        compiler_params=pltpu.CompilerParams(vmem_limit_bytes=56 << 20),
        name="invert_factor",
    )(scale, keep, tiles)


def on_device(inputs, grad_weight, counts, owners):
    samples = inputs[0]
    n = samples.shape[1]
    chip = lax.axis_index("dp")
    core = lax.axis_index("owner")
    count = lax.dynamic_slice_in_dim(counts, chip, 1)
    terms = packed_factor(samples, count)
    shares = lax.psum_scatter(terms, "dp", scatter_dimension=0, tiled=True)
    summed = lax.all_gather(shares, "dp", axis=0, tiled=True)
    scale = 1.0 / jnp.sum(counts).astype(f32)
    keep = (owners[core] == chip).astype(jnp.int32)
    inverse, kept = invert(summed, scale[None], keep[None], n)
    rows = n // lax.axis_size("dp")
    part = lax.dynamic_slice_in_dim(inverse, chip * rows, rows, 0)
    left = jnp.dot(part, grad_weight, preferred_element_type=f32)
    left = lax.ppermute(left, "owner", [(1, 0)])
    high = left.astype(bf16)
    low = (left - high.astype(f32)).astype(bf16)
    both = mm(high, inverse) + mm(low, inverse)
    both = both.astype(bf16)
    half = rows // 2
    other = lax.ppermute(both[half:], "owner", [(0, 1)])
    precond = jnp.where(core == 0, both[:half], other)
    return (kept[None, None], precond)


def solution(mesh):
    return jax.shard_map(
        on_device,
        mesh=mesh,
        in_specs=(P("owner", ("groups", "dp"), None), P("groups", None), P("groups"), P("groups")),
        out_specs=(P(("groups", "dp"), "owner", None, None), P(("groups", "dp", "owner"), None)),
        check_vma=False,
    )
```

```python
import functools
import itertools

import jax
import jax.numpy as jnp
from jax import lax
from jax.experimental import pallas as pl
from jax.experimental.pallas import tpu as pltpu
from jax.sharding import PartitionSpec as P

damping_term = 0.1
TILE = 128
LEAD = 7
f32 = jnp.float32
bf16 = jnp.bfloat16


def split3(x):
    a = x.astype(bf16)
    r = x - a.astype(f32)
    b = r.astype(bf16)
    c = (r - b.astype(f32)).astype(bf16)
    return a, b, c


def left_parts(x):
    a, b, c = split3(x)
    return jnp.concatenate([a, a, b, a, b, c], axis=1)


def right_parts(x, axis=0):
    a, b, c = split3(x)
    return jnp.concatenate([a, b, a, c, b, a], axis=axis)


def mm(a, b):
    return jnp.dot(a, b, preferred_element_type=f32)


def mm_nt(a, b):
    return lax.dot_general(a, b, (((1,), (1,)), ((), ())), preferred_element_type=f32)


def all_rows(x, p):
    return jnp.broadcast_to(x[p : p + 1, :], x.shape)


def tree_sum(xs):
    while len(xs) > 1:
        xs = [xs[i] + xs[i + 1] if i + 1 < len(xs) else xs[i] for i in range(0, len(xs), 2)]
    return xs[0]


def sweep8(M, g):
    n = M.shape[0]
    p0 = 8 * g
    lane = lax.broadcasted_iota(jnp.int32, (8, n), 1)
    sub = lax.broadcasted_iota(jnp.int32, (8, n), 0)
    inside = (lane >= p0) & (lane < p0 + 8)
    R = M[p0 : p0 + 8, :]
    V = [jnp.broadcast_to(R[:, p0 + j : p0 + j + 1], (8, n)) for j in range(8)]
    for p in range(8):
        at = sub == p
        inv = 1.0 / all_rows(V[p], p)
        Vp = jnp.where(at, -1.0, V[p])
        V = [
            Vp * inv if j == p else jnp.where(at, 0.0, V[j]) - Vp * (all_rows(V[j], p) * inv)
            for j in range(8)
        ]
    Rq = jnp.where(inside, jnp.where(lane - p0 == sub, 1.0, 0.0), -R)
    W = tree_sum([V[r] * all_rows(Rq, r) for r in range(8)])
    Wb = [all_rows(W, r) for r in range(8)]
    out = []
    for i in range(n // 8):
        if i == g:
            out.append(W)
            continue
        Mi = M[8 * i : 8 * i + 8, :]
        t = [jnp.broadcast_to(Mi[:, p0 + r : p0 + r + 1], (8, n)) * Wb[r] for r in range(8)]
        out.append(jnp.where(inside, 0.0, Mi) - tree_sum(t))
    return jnp.concatenate(out, axis=0)


def sweep_tile(M):
    for g in range(M.shape[0] // 8):
        M = sweep8(M, g)
    return M


def halves(rows):
    tiles = lambda some: [(i, j) for i in some for j in range(i + 1)]
    whole = len(tiles(rows))
    for k in range(1, len(rows)):
        for some in itertools.combinations(rows, k):
            if 2 * len(tiles(some)) == whole:
                return tiles(some), tiles([i for i in rows if i not in some])
    raise ValueError("no halves")


def tile_at(t):
    return slice(t * TILE, (t + 1) * TILE)


def mask_kernel(count_ref, x_ref, lead_ref, rest_ref):
    x = x_ref[...]
    live = lax.broadcasted_iota(jnp.int32, x.shape, 0) < count_ref[0]
    x = jnp.where(live, x, jnp.zeros_like(x))
    cut = lead_ref.shape[1]
    lead_ref[...] = x[:, :cut]
    rest_ref[...] = x[:, cut:]


def terms_kernel(rows, parts, chunks, y_ref, *refs):
    lead, refs = refs[:parts], refs[parts:]
    if rows[0] > 0:
        rest, refs = refs[:parts], refs[parts:]
    sends, refs = refs[: len(chunks)], refs[len(chunks) :]
    keep, X, XT, buf = refs
    at = 0
    cut = lead[0].shape[1]
    for p in range(parts):
        h = lead[p].shape[0]
        here = slice(at, at + h)
        X[here, :cut] = lead[p][...]
        if rows[0] > 0:
            X[here, cut:] = rest[p][...]
            XT[:, here] = rest[p][...].T
        else:
            XT[:, here] = lead[p][...].T
        at += h
    first, second = halves(rows)
    half = len(first)
    order = first + second
    for i in rows:
        r = i - rows[0]
        panel = mm(XT[tile_at(r), :], X[:, : (i + 1) * TILE])
        for j in range(i + 1):
            buf[tile_at(order.index((i, j))), :] = panel[:, tile_at(j)]
    low = y_ref[0] == 0
    at = 0
    for send in sends:
        for t in range(send.shape[0] // TILE):
            a, b = buf[tile_at(at), :], buf[tile_at(half + at), :]
            send[tile_at(t), :] = jnp.where(low, a, b)
            keep[tile_at(at), :] = jnp.where(low, b, a)
            at += 1


def packed_kernel(x_ref, out_ref):
    x = x_ref[...]
    xt = x.T
    at = 0
    for i in range(x.shape[1] // TILE):
        panel = mm(xt[tile_at(i), :], x[:, : (i + 1) * TILE])
        for j in range(i + 1):
            out_ref[tile_at(at), :] = panel[:, tile_at(j)]
            at += 1


def summed_tiles(rows, chunks, y_ref, refs):
    if chunks is None:
        (packed,) = refs
        return lambda i, j: packed[tile_at(i * (i + 1) // 2 + j), :]
    count = len(chunks)
    sends, near, far, near_other, far_other = (refs[count * q : count * (q + 1)] for q in range(5))
    keep = refs[5 * count]
    first, second = halves(rows)
    where = [(c, t) for c in range(count) for t in range(chunks[c])]
    low = y_ref[0] == 0

    def tile(i, j):
        side = 0 if (i, j) in first else 1
        t = (second if side else first).index((i, j))
        c, u = where[t]
        u = tile_at(u)
        mine = sends[c][u, :] + (near[c][u, :] + far[c][u, :])
        other = keep[tile_at(t), :] + (near_other[c][u, :] + far_other[c][u, :])
        return jnp.where(low, other, mine) if side else jnp.where(low, mine, other)

    return tile


def damped_tile(tile, i, j, scale):
    t = tile(i, j) * scale
    if i == j:
        row = lax.broadcasted_iota(jnp.int32, (TILE, TILE), 0)
        column = lax.broadcasted_iota(jnp.int32, (TILE, TILE), 1)
        t = t + jnp.where(row == column, damping_term, 0.0)
    return t


def lead_kernel(chunks, y_ref, scale_ref, *refs):
    *sources, A, N = refs
    tile = summed_tiles(range(LEAD), chunks, y_ref, sources)
    scale = scale_ref[0]
    for i in range(LEAD):
        for j in range(i + 1):
            t = damped_tile(tile, i, j, scale)
            A[tile_at(i), tile_at(j)] = t
            if i == 0:
                N[...] = sweep_tile(t)
            if i != j:
                A[tile_at(j), tile_at(i)] = t.T


def step_kernel(k, m, last, a_ref, n_ref, *refs):
    if last:
        A, Cs, Ws, Wf = refs
    else:
        A, N, Cs, Ws, Wf = refs
    here = tile_at(k)
    D = n_ref[...]
    Nl = left_parts(D)
    Nr = right_parts(D)
    if not last:
        later = tile_at(k + 1)
        Wn = mm(Nl, right_parts(A[here, later]))
        T = A[later, later] + mm(left_parts(A[later, here]), right_parts(Wn))
        N[...] = sweep_tile(T)
    sweep_rest(A, here, m, D, Nl, Nr, Cs, Ws, Wf)


def sweep_rest(A, here, m, D, Nl, Nr, Cs, Ws, Wf):
    wide = 2 * TILE
    for c in range(0, m, wide):
        w = min(wide, m - c)
        Wc = mm(Nl, right_parts(A[here, c : c + w]))
        Wf[:, c : c + w] = Wc
        Ws[:, c : c + w] = right_parts(Wc)
    for r in range(0, m, wide):
        h = min(wide, m - r)
        Cs[r : r + h, :] = left_parts(A[r : r + h, here])
    for c in range(0, m, wide):
        w = min(wide, m - c)
        A[:m, c : c + w] = A[:m, c : c + w] + mm(Cs[:m, :], Ws[:, c : c + w])
    A[:m, here] = -mm(Cs[:m, :], Nr)
    A[here, :m] = -Wf[:, :m]
    A[here, here] = D


def mm6(x, y, dot):
    pairs = ((0, 2), (1, 1), (2, 0), (0, 1), (1, 0), (0, 0))
    return functools.reduce(lambda s, t: s + t, [dot(x[i], y[j]) for i, j in pairs])


def merge_kernel(chunks, y_ref, scale_ref, a_ref, *refs):
    *sources, A, N, Qs, Ps = refs
    n = A.shape[0]
    m = LEAD * TILE
    blocks = n // TILE
    tile = summed_tiles(range(LEAD, blocks), chunks, y_ref, sources)
    scale = scale_ref[0]
    for c in range(0, m, 2 * TILE):
        w = min(2 * TILE, m - c)
        for q, part in enumerate(split3(A[:m, c : c + w])):
            Ps[q, :, c : c + w] = part
    for i in range(LEAD, blocks):
        r = tile_at(i - LEAD)
        row = split3(jnp.concatenate([damped_tile(tile, i, j, scale) for j in range(LEAD)], axis=1))
        for q, part in enumerate(row):
            Qs[q, r, :] = part
        W = -mm6(row, Ps, mm)
        A[tile_at(i), :m] = W
        W3 = split3(W)
        for j in range(LEAD, i + 1):
            t = damped_tile(tile, i, j, scale)
            t = t - mm6(W3, [Qs[q, tile_at(j - LEAD), :] for q in range(3)], mm_nt)
            A[tile_at(i), tile_at(j)] = t
            if i == LEAD:
                N[...] = sweep_tile(t)
            if i != j:
                A[tile_at(j), tile_at(i)] = t.T
        for j in range(LEAD):
            A[tile_at(j), tile_at(i)] = W[:, tile_at(j)].T


def last_kernel(keep_ref, a_ref, n_ref, inv_ref, kept_ref, A, Cs, Ws, Wf):
    n = inv_ref.shape[0]
    blocks = n // TILE
    D = n_ref[...]
    sweep_rest(A, tile_at(blocks - 1), n, D, left_parts(D), right_parts(D), Cs, Ws, Wf)
    keep = keep_ref[0] != 0
    for i in range(blocks):
        r = (-A[tile_at(i), :]).astype(bf16)
        inv_ref[tile_at(i), :] = r
        kept_ref[tile_at(i), :] = jnp.where(keep, r, jnp.zeros_like(r))


vmem = lambda: pl.BlockSpec(memory_space=pltpu.VMEM)
smem = lambda: pl.BlockSpec(memory_space=pltpu.SMEM)


def call(kernel, name, scalars, arrays, outs, scratch=(), aliases=None, us=5, limit=48):
    out = pl.pallas_call(
        kernel,
        out_shape=[jax.ShapeDtypeStruct(s, d) for s, d in outs],
        in_specs=[smem()] * len(scalars) + [vmem()] * len(arrays),
        out_specs=[vmem()] * len(outs),
        scratch_shapes=[pltpu.VMEM(s, d) for s, d in scratch],
        input_output_aliases={len(scalars) + a: b for a, b in (aliases or {}).items()},
        compiler_params=pltpu.CompilerParams(vmem_limit_bytes=limit << 20),
        cost_estimate=pl.CostEstimate(flops=int(us * 1.1e9), bytes_accessed=0, transcendentals=0),
        name=name,
    )(*scalars, *arrays)
    return out


def panel_scratch(m):
    return [((m, 6 * TILE), bf16), ((6 * TILE, m), bf16), ((TILE, m), f32)]


def sweep_step(A, N, k, m):
    n = A.shape[0]
    last = (k + 1) * TILE == m
    outs = [((n, n), f32)] + ([] if last else [((TILE, TILE), f32)])
    aliases = {0: 0} if last else {0: 0, 1: 1}
    out = call(
        functools.partial(step_kernel, k, m, last),
        "sweep_%d" % k,
        [],
        [A, N],
        outs,
        panel_scratch(m),
        aliases,
        us=2 if last else 5,
        limit=24,
    )
    return out if not last else (out[0], None)


def gather4(x):
    rows = x.shape[0] // 2
    z_pair = [(2 * z + y, 2 * (z ^ 1) + y) for z in range(4) for y in range(2)]
    y_pair = [(i, i ^ 1) for i in range(8)]
    across = lax.ppermute(x, "dp", y_pair)
    along = lax.ppermute(x, "dp", z_pair)
    corner_a = lax.ppermute(across[:rows], "dp", z_pair)
    corner_b = lax.ppermute(along[rows:], "dp", y_pair)
    return [x, across, along, corner_a, corner_b]


def exchange(sends):
    middle = [(2 * z + y, 2 * (3 - z) + y) for z in (1, 2) for y in range(2)]
    outward = [(2 * a + y, 2 * b + y) for a, b in ((1, 0), (2, 3)) for y in range(2)]
    swap_middle = [(2 * z + y, 2 * z + 1 - y) for z in (1, 2) for y in range(2)]
    swap_end = [(2 * z + y, 2 * z + 1 - y) for z in (0, 3) for y in range(2)]
    near = [lax.ppermute(s, "dp", middle) for s in sends]
    far = [lax.ppermute(s, "dp", outward) for s in near]
    near_other = [lax.ppermute(s, "dp", swap_middle) for s in near]
    far_other = [lax.ppermute(s, "dp", swap_end) for s in far]
    return near, far, near_other, far_other


def terms(rows, parts, chunks, y, n, name):
    lead, rest = parts
    tokens = sum(p.shape[0] for p in lead)
    count = sum(chunks)
    width = (rows[-1] + 1) * TILE
    out = call(
        functools.partial(terms_kernel, rows, len(lead), chunks),
        name,
        [y],
        lead + rest,
        [((c * TILE, TILE), f32) for c in chunks] + [((count * TILE, TILE), f32)],
        [
            ((tokens, width), bf16),
            ((len(rows) * TILE, tokens), bf16),
            ((2 * count * TILE, TILE), f32),
        ],
        us=4,
    )
    return out[:-1], out[-1]


def on_device(inputs, grad_weight, counts, owners):
    samples = inputs[0]
    n = samples.shape[1]
    blocks = n // TILE
    m = LEAD * TILE
    chip = lax.axis_index("dp")
    core = lax.axis_index("owner")
    count = lax.dynamic_slice_in_dim(counts, chip, 1)
    scale = (1.0 / jnp.sum(counts).astype(f32))[None]
    keep = (owners[core] == chip).astype(jnp.int32)[None]
    y = (chip % 2).astype(jnp.int32)[None]
    tok = samples.shape[0]
    lead, rest = call(
        mask_kernel, "mask_tokens", [count], [samples], [((tok, m), bf16), ((tok, n - m), bf16)], us=1
    )
    if lax.axis_size("dp") == 8:
        lead_chunks, rest_chunks = (7, 7), (7, 6, 6)
        leads = gather4(lead)
        rest = lax.optimization_barrier((rest, leads[3], leads[4]))[0]
        lead_sends, lead_keep = terms(range(LEAD), (leads, []), lead_chunks, y, n, "lead_terms")
        rests = gather4(rest)
        lead_got = exchange(lead_sends)
        rest_sends, rest_keep = terms(
            range(LEAD, blocks), (leads, rests), rest_chunks, y, n, "rest_terms"
        )
        rest_got = exchange(rest_sends)
        lead_src = list(lead_sends) + sum(lead_got, []) + [lead_keep]
        rest_src = list(rest_sends) + sum(rest_got, []) + [rest_keep]
    else:
        lead_chunks = rest_chunks = None
        whole = jnp.concatenate([lead, rest], axis=1)
        tiles = blocks * (blocks + 1) // 2
        packed = call(packed_kernel, "own_terms", [], [whole], [((tiles * TILE, TILE), f32)])[0]
        shares = lax.psum_scatter(packed, "dp", scatter_dimension=0, tiled=True)
        lead_src = rest_src = [lax.all_gather(shares, "dp", axis=0, tiled=True)]
    A, N = call(
        functools.partial(lead_kernel, lead_chunks),
        "lead_tiles",
        [y, scale],
        lead_src,
        [((n, n), f32), ((TILE, TILE), f32)],
        us=6,
        limit=20,
    )
    for k in range(LEAD):
        A, N = sweep_step(A, N, k, m)
    w = n - m
    A, N = call(
        functools.partial(merge_kernel, rest_chunks),
        "rest_tiles",
        [y, scale],
        [A] + rest_src,
        [((n, n), f32), ((TILE, TILE), f32)],
        [((3, w, m), bf16), ((3, m, m), bf16)],
        {0: 0},
        us=9,
        limit=36,
    )
    for k in range(LEAD, blocks - 1):
        A, N = sweep_step(A, N, k, n)
    inverse, kept, _ = call(
        last_kernel,
        "sweep_last",
        [keep],
        [A, N],
        [((n, n), bf16)] * 2 + [((n, n), f32)],
        panel_scratch(n),
        {0: 2},
        us=5,
        limit=32,
    )
    rows = n // lax.axis_size("dp")
    part = lax.dynamic_slice_in_dim(inverse, chip * rows, rows, 0)
    left = jnp.dot(part, grad_weight, preferred_element_type=f32)
    left = lax.ppermute(left, "owner", [(1, 0)])
    high = left.astype(bf16)
    low = (left - high.astype(f32)).astype(bf16)
    both = (mm(high, inverse) + mm(low, inverse)).astype(bf16)
    half = rows // 2
    other = lax.ppermute(both[half:], "owner", [(0, 1)])
    precond = jnp.where(core == 0, both[:half], other)
    return (kept[None, None], precond)


def solution(mesh):
    return jax.shard_map(
        on_device,
        mesh=mesh,
        in_specs=(P("owner", ("groups", "dp"), None), P("groups", None), P("groups"), P("groups")),
        out_specs=(P(("groups", "dp"), "owner", None, None), P(("groups", "dp", "owner"), None)),
        check_vma=False,
    )
```

```python
import functools

import jax
import jax.numpy as jnp
from jax import lax
from jax.experimental import pallas as pl
from jax.experimental.pallas import tpu as pltpu
from jax.sharding import PartitionSpec as P

damping_term = 0.1
TILE = 128
LEAD = 7
f32 = jnp.float32
bf16 = jnp.bfloat16


def split3(x):
    a = x.astype(bf16)
    r = x - a.astype(f32)
    b = r.astype(bf16)
    c = (r - b.astype(f32)).astype(bf16)
    return a, b, c


def left_parts(x):
    a, b, c = split3(x)
    return jnp.concatenate([a, a, b, a, b, c], axis=1)


def right_parts(x, axis=0):
    a, b, c = split3(x)
    return jnp.concatenate([a, b, a, c, b, a], axis=axis)


def mm(a, b):
    return jnp.dot(a, b, preferred_element_type=f32)


def mm_nt(a, b):
    return lax.dot_general(a, b, (((1,), (1,)), ((), ())), preferred_element_type=f32)


def all_rows(x, p):
    return jnp.broadcast_to(x[p : p + 1, :], x.shape)


def tree_sum(xs):
    while len(xs) > 1:
        xs = [xs[i] + xs[i + 1] if i + 1 < len(xs) else xs[i] for i in range(0, len(xs), 2)]
    return xs[0]


def sweep8(M, g):
    n = M.shape[0]
    p0 = 8 * g
    lane = lax.broadcasted_iota(jnp.int32, (8, n), 1)
    sub = lax.broadcasted_iota(jnp.int32, (8, n), 0)
    inside = (lane >= p0) & (lane < p0 + 8)
    R = M[p0 : p0 + 8, :]
    V = [jnp.broadcast_to(R[:, p0 + j : p0 + j + 1], (8, n)) for j in range(8)]
    for p in range(8):
        at = sub == p
        inv = 1.0 / all_rows(V[p], p)
        Vp = jnp.where(at, -1.0, V[p])
        V = [
            Vp * inv if j == p else jnp.where(at, 0.0, V[j]) - Vp * (all_rows(V[j], p) * inv)
            for j in range(8)
        ]
    Rq = jnp.where(inside, jnp.where(lane - p0 == sub, 1.0, 0.0), -R)
    W = tree_sum([V[r] * all_rows(Rq, r) for r in range(8)])
    Wb = [all_rows(W, r) for r in range(8)]
    out = []
    for i in range(n // 8):
        if i == g:
            out.append(W)
            continue
        Mi = M[8 * i : 8 * i + 8, :]
        t = [jnp.broadcast_to(Mi[:, p0 + r : p0 + r + 1], (8, n)) * Wb[r] for r in range(8)]
        out.append(jnp.where(inside, 0.0, Mi) - tree_sum(t))
    return jnp.concatenate(out, axis=0)


def sweep_tile(M):
    for g in range(M.shape[0] // 8):
        M = sweep8(M, g)
    return M


def halves(rows):
    tiles = [(i, j) for i in rows for j in range(i + 1)]
    cut = (len(tiles) + 1) // 2
    return tiles[:cut], tiles[cut:] + tiles[-1:] * (2 * cut - len(tiles))


def chunked(total, count):
    return tuple((total + count - 1 - c) // count for c in range(count))


def tile_at(t):
    return slice(t * TILE, (t + 1) * TILE)


def mask_kernel(counts_ref, x_ref, lead_ref, rest_ref):
    x = x_ref[...]
    live = lax.broadcasted_iota(jnp.int32, x.shape, 0) < counts_ref[lax.axis_index("dp")]
    x = jnp.where(live, x, jnp.zeros_like(x))
    cut = lead_ref.shape[1]
    lead_ref[...] = x[:, :cut]
    rest_ref[...] = x[:, cut:]


def terms_kernel(rows, parts, chunks, *refs):
    lead, refs = refs[:parts], refs[parts:]
    if rows[0] > 0:
        rest, refs = refs[:parts], refs[parts:]
    sends, refs = refs[: len(chunks)], refs[len(chunks) :]
    keep, X, XT, buf = refs
    at = 0
    cut = lead[0].shape[1]
    for p in range(parts):
        h = lead[p].shape[0]
        here = slice(at, at + h)
        X[here, :cut] = lead[p][...]
        if rows[0] > 0:
            X[here, cut:] = rest[p][...]
            XT[:, here] = rest[p][...].T
        else:
            XT[:, here] = lead[p][...].T
        at += h
    first, second = halves(rows)
    half = len(first)
    order = first + second
    for i in rows:
        r = i - rows[0]
        panel = mm(XT[tile_at(r), :], X[:, : (i + 1) * TILE])
        for t, (a, j) in enumerate(order):
            if a == i:
                buf[tile_at(t), :] = panel[:, tile_at(j)]
    low = lax.axis_index("dp") % 2 == 0
    at = 0
    for send in sends:
        for t in range(send.shape[0] // TILE):
            a, b = buf[tile_at(at), :], buf[tile_at(half + at), :]
            send[tile_at(t), :] = jnp.where(low, a, b)
            keep[tile_at(at), :] = jnp.where(low, b, a)
            at += 1


def packed_kernel(x_ref, out_ref):
    x = x_ref[...]
    xt = x.T
    at = 0
    for i in range(x.shape[1] // TILE):
        panel = mm(xt[tile_at(i), :], x[:, : (i + 1) * TILE])
        for j in range(i + 1):
            out_ref[tile_at(at), :] = panel[:, tile_at(j)]
            at += 1


def summed_tiles(rows, chunks, refs):
    if chunks is None:
        (packed,) = refs
        return (lambda i, j: packed[tile_at(i * (i + 1) // 2 + j), :]), lambda: None
    count = len(chunks)
    sends, near, far, near_other, far_other = (refs[count * q : count * (q + 1)] for q in range(5))
    keep, got, sems = refs[5 * count :]
    first, second = halves(rows)
    half = len(first)
    line = lax.axis_index("dp") // 2
    middle = (line == 1) | (line == 2)
    waits = []
    at = 0
    for q, (inner, outer) in enumerate(((near, far), (near_other, far_other))):
        for c in range(count):
            size = chunks[c] * TILE
            to = got.at[pl.ds(at, size), :]
            at += size
            sem = sems.at[q * count + c]

            @pl.when(middle)
            def _(src=inner[c], to=to, sem=sem):
                pltpu.make_async_copy(src, to, sem).start()

            @pl.when(jnp.logical_not(middle))
            def _(src=outer[c], to=to, sem=sem):
                pltpu.make_async_copy(src, to, sem).start()

            waits.append(pltpu.make_async_copy(inner[c], to, sem))
    where = [(c, t) for c in range(count) for t in range(chunks[c])]
    low = lax.axis_index("dp") % 2 == 0

    def tile(i, j):
        side = 0 if (i, j) in first else 1
        t = (second if side else first).index((i, j))
        c, u = where[t]
        mine = sends[c][tile_at(u), :] + got[tile_at(t), :]
        other = keep[tile_at(t), :] + got[tile_at(half + t), :]
        return jnp.where(low, other, mine) if side else jnp.where(low, mine, other)

    def arrive():
        for w in waits:
            w.wait()

    return tile, arrive


def damped_tile(tile, i, j, scale):
    t = tile(i, j) * scale
    if i == j:
        row = lax.broadcasted_iota(jnp.int32, (TILE, TILE), 0)
        column = lax.broadcasted_iota(jnp.int32, (TILE, TILE), 1)
        t = t + jnp.where(row == column, damping_term, 0.0)
    return t


def lead_kernel(chunks, scale_ref, *refs):
    count = 1 if chunks is None else 5 * len(chunks) + 1
    sources, (A, N), sources2 = refs[:count], refs[count : count + 2], refs[count + 2 :]
    tile, arrive = summed_tiles(range(LEAD), chunks, sources + sources2)
    arrive()
    scale = scale_ref[0]
    for i in range(LEAD):
        for j in range(i + 1):
            t = damped_tile(tile, i, j, scale)
            A[tile_at(i), tile_at(j)] = t
            if i == 0:
                N[...] = sweep_tile(t)
            if i != j:
                A[tile_at(j), tile_at(i)] = t.T


def step_kernel(k, last, a_ref, n_ref, *refs):
    if last:
        A, Cs, Ws, Wf = refs
        sweep(A, n_ref, None, tile_at(k), None, Cs, Ws, Wf)
    else:
        A, N, Cs, Ws, Wf = refs
        sweep(A, n_ref, N, tile_at(k), tile_at(k + 1), Cs, Ws, Wf)


def sweep(A, D_ref, N, here, later, Cs, Ws, Wf):
    m = A.shape[0]
    D = D_ref[...]
    Nl = left_parts(D)
    Nr = right_parts(D)
    if later is not None:
        Wn = mm(Nl, right_parts(A[here, later]))
        T = A[later, later] + mm(left_parts(A[later, here]), right_parts(Wn))
        N[...] = sweep_tile(T)
    wide = 2 * TILE
    for c in range(0, m, wide):
        w = min(wide, m - c)
        Wc = mm(Nl, right_parts(A[here, c : c + w]))
        Wf[:, c : c + w] = Wc
        Ws[:, c : c + w] = right_parts(Wc)
    for r in range(0, m, wide):
        h = min(wide, m - r)
        Cs[r : r + h, :] = left_parts(A[r : r + h, here])
    for c in range(0, m, wide):
        w = min(wide, m - c)
        A[:, c : c + w] = A[:, c : c + w] + mm(Cs[...], Ws[:, c : c + w])
    A[:, here] = -mm(Cs[...], Nr)
    A[here, :] = -Wf[...]
    A[here, here] = D


def mm6(x, y, dot):
    pairs = ((0, 2), (1, 1), (2, 0), (0, 1), (1, 0), (0, 0))
    return functools.reduce(lambda s, t: s + t, [dot(x[i], y[j]) for i, j in pairs])


def merge_kernel(chunks, own_rows, scale_ref, keep_ref, lead_ref, *refs):
    count = 1 if chunks is None else 5 * len(chunks) + 1
    sources, refs = refs[:count], refs[count:]
    if own_rows:
        grad_ref, inv_ref, kept_ref, left_ref, *refs = refs
    else:
        inv_ref, kept_ref, *refs = refs
    A, N, Qs, Ps, Cs, Ws, Wf, kept = refs[:8]
    *more, sems = refs[8:]
    n = A.shape[0]
    m = LEAD * TILE
    blocks = n // TILE
    if chunks is not None:
        more.append(sems.at[pl.ds(4, 2 * len(chunks))])
    tile, arrive = summed_tiles(range(LEAD, blocks), chunks, sources + tuple(more))
    scale = scale_ref[0]
    for c in range(0, m, 2 * TILE):
        w = min(2 * TILE, m - c)
        lead = lead_ref[:, c : c + w]
        A[:m, c : c + w] = lead
        for q, part in enumerate(split3(lead)):
            Ps[q, :, c : c + w] = part
    arrive()
    for some in (range(LEAD, LEAD + 1), range(LEAD + 1, blocks)):
        for i in some:
            for j in range(LEAD):
                for q, part in enumerate(split3(damped_tile(tile, i, j, scale))):
                    Qs[q, tile_at(i - LEAD), tile_at(j)] = part
        rows = slice((some[0] - LEAD) * TILE, (some[-1] + 1 - LEAD) * TILE)
        W = -mm6([Qs[q, rows, :] for q in range(3)], Ps, mm)
        A[some[0] * TILE : (some[-1] + 1) * TILE, :m] = W
        W3 = split3(W)
        width = (some[-1] + 1 - LEAD) * TILE
        S = mm6(W3, [Qs[q, :width, :] for q in range(3)], mm_nt)
        for i in some:
            r = tile_at(i - some[0])
            for j in range(LEAD, i + 1):
                t = damped_tile(tile, i, j, scale) - S[r, tile_at(j - LEAD)]
                A[tile_at(i), tile_at(j)] = t
                if i == LEAD:
                    N[...] = sweep_tile(t)
                if i != j:
                    A[tile_at(j), tile_at(i)] = t.T
            for j in range(LEAD):
                A[tile_at(j), tile_at(i)] = W[r, tile_at(j)].T

    def step(k, _):
        here = pl.ds(pl.multiple_of(k * TILE, TILE), TILE)
        later = pl.ds(pl.multiple_of((k + 1) * TILE, TILE), TILE)
        sweep(A, N, N, here, later, Cs, Ws, Wf)
        return 0

    lax.fori_loop(LEAD, blocks - 1, step, 0)
    here = tile_at(blocks - 1)
    D = N[...]
    Nl = left_parts(D)
    Nr = right_parts(D)
    keep = keep_ref[0] != 0
    wide = 2 * TILE
    for c in range(0, n, wide):
        w = min(wide, n - c)
        Wc = mm(Nl, right_parts(A[here, c : c + w]))
        Wf[:, c : c + w] = Wc
        Ws[:, c : c + w] = right_parts(Wc)
    tall = n // 4
    copies = []
    for q in range(4):
        rows = slice(q * tall, (q + 1) * tall)
        C = left_parts(A[rows, here])
        for c in range(0, n - TILE, wide):
            w = min(wide, n - TILE - c)
            r = -(A[rows, c : c + w] + mm(C, Ws[:, c : c + w]))
            inv_ref[rows, c : c + w] = r.astype(bf16)
        inv_ref[rows, here] = mm(C, Nr).astype(bf16)
        if q == 3:
            inv_ref[here, :] = Wf[...].astype(bf16)
            inv_ref[here, here] = (-D).astype(bf16)
        r = inv_ref[rows, :]
        kept[rows, :] = jnp.where(keep, r, jnp.zeros_like(r))
        copy = pltpu.make_async_copy(kept.at[rows, :], kept_ref.at[rows, :], sems.at[q])
        copy.start()
        copies.append(copy)
    if own_rows:
        at = pl.multiple_of(lax.axis_index("dp") * own_rows, 16)
        left_ref[...] = mm(inv_ref[pl.ds(at, own_rows), :], grad_ref[...])
    for copy in copies:
        copy.wait()


def finish_kernel(left_ref, inv_ref, out_ref):
    left = left_ref[...]
    high = left.astype(bf16)
    low = (left - high.astype(f32)).astype(bf16)
    both = mm(jnp.concatenate([high, low], axis=0), inv_ref[...])
    rows = left.shape[0]
    out_ref[...] = (both[:rows] + both[rows:]).astype(bf16)


vmem = lambda: pl.BlockSpec(memory_space=pltpu.VMEM)
smem = lambda: pl.BlockSpec(memory_space=pltpu.SMEM)


def call(kernel, name, scalars, arrays, outs, scratch=(), aliases=None, us=5, limit=36, anys=(), any_outs=(), sems=0):
    anywhere = pl.BlockSpec(memory_space=pl.ANY)
    out = pl.pallas_call(
        kernel,
        out_shape=[jax.ShapeDtypeStruct(*o) for o in outs],
        in_specs=[smem()] * len(scalars) + [anywhere if a in anys else vmem() for a in range(len(arrays))],
        out_specs=[anywhere if a in any_outs else vmem() for a in range(len(outs))],
        scratch_shapes=[pltpu.VMEM(s, d) for s, d in scratch]
        + ([pltpu.SemaphoreType.DMA((sems,))] if sems else []),
        input_output_aliases={len(scalars) + a: b for a, b in (aliases or {}).items()},
        compiler_params=pltpu.CompilerParams(vmem_limit_bytes=limit << 20),
        cost_estimate=pl.CostEstimate(flops=int(us * 1.1e9), bytes_accessed=0, transcendentals=0),
        name=name,
    )(*scalars, *arrays)
    return out


def panel_scratch(m):
    return [((m, 6 * TILE), bf16), ((6 * TILE, m), bf16), ((TILE, m), f32)]


def sweep_step(A, N, k):
    m = A.shape[0]
    last = (k + 1) * TILE == m
    out = call(
        functools.partial(step_kernel, k, last),
        "sweep_%d" % k,
        [],
        [A, N],
        [((m, m), f32)] + ([] if last else [((TILE, TILE), f32)]),
        panel_scratch(m),
        {0: 0} if last else {0: 0, 1: 1},
        us=5,
        limit=16,
    )
    return (out[0], None) if last else out


Z_PAIR = [(2 * z + y, 2 * (z ^ 1) + y) for z in range(4) for y in range(2)]
Y_PAIR = [(i, i ^ 1) for i in range(8)]


def neighbours(x):
    return hop(x, Y_PAIR), hop(x, Z_PAIR)


def corner(across, along):
    rows = across.shape[0] // 2
    return hop(across[:rows], Z_PAIR), hop(along[rows:], Y_PAIR)


MIDDLE = [(2 * z + y, 2 * (3 - z) + y) for z in (1, 2) for y in range(2)]
OUTWARD = [(2 * a + y, 2 * b + y) for a, b in ((1, 0), (2, 3)) for y in range(2)]
SWAP_MIDDLE = [(2 * z + y, 2 * z + 1 - y) for z in (1, 2) for y in range(2)]
SWAP_END = [(2 * z + y, 2 * z + 1 - y) for z in (0, 3) for y in range(2)]


def hop(x, pairs):
    return lax.ppermute(x, "dp", pairs)


def terms(rows, parts, chunks, name):
    lead, rest = parts
    tokens = sum(p.shape[0] for p in lead)
    count = sum(chunks)
    width = (rows[-1] + 1) * TILE
    out = call(
        functools.partial(terms_kernel, rows, len(lead), chunks),
        name,
        [],
        lead + rest,
        [((c * TILE, TILE), f32) for c in chunks] + [((count * TILE, TILE), f32)],
        [
            ((tokens, width), bf16),
            ((len(rows) * TILE, tokens), bf16),
            ((2 * count * TILE, TILE), f32),
        ],
        us=4,
    )
    return out[:-1], out[-1]


def tie(*xs):
    return lax.optimization_barrier(xs)


def on_device(inputs, grad_weight, counts, owners):
    samples = inputs[0]
    n = samples.shape[1]
    blocks = n // TILE
    m = LEAD * TILE
    w = n - m
    chip = lax.axis_index("dp")
    core = lax.axis_index("owner")
    tok = samples.shape[0]
    lead, rest = call(
        mask_kernel, "mask_tokens", [counts], [samples], [((tok, m), bf16), ((tok, w), bf16)], us=1
    )
    scale = (1.0 / jnp.sum(counts).astype(f32))[None]
    keep = (owners[core] == chip).astype(jnp.int32)[None]
    dma = lambda k, at: dict(anys=range(at + k, at + 5 * k), sems=2 * k)
    if lax.axis_size("dp") == 8:
        lead_chunks = chunked(len(halves(range(LEAD))[0]), 2)
        rest_chunks = chunked(len(halves(range(LEAD, blocks))[0]), 3)
        across, along = neighbours(lead)
        leads = [lead, across, along, *corner(across, along)]
        rest = tie(rest, leads[3], leads[4])[0]
        lead_sends, lead_keep = terms(range(LEAD), (leads, []), lead_chunks, "lead_terms")
        near = [hop(x, MIDDLE) for x in lead_sends]
        across, along = neighbours(rest)
        far = [hop(x, OUTWARD) for x in near]
        near_other = [hop(x, SWAP_MIDDLE) for x in near]
        across, along, near[1], far[0] = tie(across, along, near[1], far[0])
        far_other = [hop(x, SWAP_END) for x in far]
        *diagonal, far[1] = tie(*corner(across, along), far[1])
        lead_got = near, far, near_other, far_other
        rest_sends, rest_keep = terms(
            range(LEAD, blocks), (leads, [rest, across, along, *diagonal]), rest_chunks, "rest_terms"
        )
        near = [hop(x, MIDDLE) for x in rest_sends]
        lead_src = list(lead_sends) + sum(lead_got, []) + [lead_keep]
        lead_dma = dma(len(lead_chunks), 0)
        rest_dma = dma(len(rest_chunks), 1)
        rest_dma["sems"] += 4
        lead_buf = [((2 * sum(lead_chunks) * TILE, TILE), f32)]
        rest_buf = [((2 * sum(rest_chunks) * TILE, TILE), f32)]
    else:
        lead_chunks = rest_chunks = None
        lead_dma, rest_dma = {}, dict(sems=4)
        lead_buf = rest_buf = []
        whole = jnp.concatenate([lead, rest], axis=1)
        tiles = blocks * (blocks + 1) // 2
        packed = call(packed_kernel, "own_terms", [], [whole], [((tiles * TILE, TILE), f32)])[0]
        shares = lax.psum_scatter(packed, "dp", scatter_dimension=0, tiled=True)
        lead_src = rest_src = [lax.all_gather(shares, "dp", axis=0, tiled=True)]
    A, N = call(
        functools.partial(lead_kernel, lead_chunks),
        "lead_tiles",
        [scale],
        lead_src,
        [((m, m), f32), ((TILE, TILE), f32)],
        lead_buf,
        us=0.05,
        limit=16,
        **lead_dma,
    )
    passes = {} if rest_chunks is None else {-1: 0, 1: 1, 2: 2}
    swaps = {} if rest_chunks is None else {1: 0, 3: 1, 4: 2}
    far, near_other, far_other = {}, {}, {}
    for k in range(-1, LEAD):
        if k >= 0:
            A, N = sweep_step(A, N, k)
        if k in passes:
            c = passes[k]
            N, near[c] = tie(N, near[c])
            far[c] = hop(near[c], OUTWARD)
            near_other[c] = hop(near[c], SWAP_MIDDLE)
        if k in swaps:
            c = swaps[k]
            N, far[c] = tie(N, far[c])
            far_other[c] = hop(far[c], SWAP_END)
    if rest_chunks is not None:
        count = range(len(rest_chunks))
        parts = [near] + [[d[c] for c in count] for d in (far, near_other, far_other)]
        rest_src = list(rest_sends) + sum(parts, []) + [rest_keep]
    tile = ((TILE, TILE), f32)
    rows = n // lax.axis_size("dp")
    fused = rows % 16 == 0
    inverse, kept, *left = call(
        functools.partial(merge_kernel, rest_chunks, rows if fused else 0),
        "rest_tiles",
        [scale, keep],
        [A] + rest_src + ([grad_weight] if fused else []),
        [((n, n), bf16)] * 2 + ([((rows, n), f32)] if fused else []),
        [((n, n), f32), tile, ((3, w, m), bf16), ((3, m, m), bf16)]
        + panel_scratch(n)
        + [((n, n), bf16)]
        + rest_buf,
        us=30,
        limit=44,
        any_outs=(1,),
        **rest_dma,
    )
    if fused:
        left = left[0]
    else:
        part = lax.dynamic_slice_in_dim(inverse, chip * rows, rows, 0)
        left = jnp.dot(part, grad_weight, preferred_element_type=f32)
    left = lax.ppermute(left, "owner", [(1, 0)])
    both = call(finish_kernel, "finish", [], [left, inverse], [((rows, n), bf16)], us=1, limit=36)[0]
    half = rows // 2
    other = lax.ppermute(both[half:], "owner", [(0, 1)])
    precond = jnp.where(core == 0, both[:half], other)
    return (kept[None, None], precond)


def solution(mesh):
    return jax.shard_map(
        on_device,
        mesh=mesh,
        in_specs=(P("owner", ("groups", "dp"), None), P("groups", None), P("groups"), P("groups")),
        out_specs=(P(("groups", "dp"), "owner", None, None), P(("groups", "dp", "owner"), None)),
        check_vma=False,
    )
```

```python
import functools

import jax
import jax.numpy as jnp
from jax import lax
from jax.experimental import pallas as pl
from jax.experimental.pallas import tpu as pltpu
from jax.sharding import PartitionSpec as P

damping_term = 0.1
TILE = 128
LEAD = 7
f32 = jnp.float32
bf16 = jnp.bfloat16


def split3(x):
    a = x.astype(bf16)
    r = x - a.astype(f32)
    b = r.astype(bf16)
    c = (r - b.astype(f32)).astype(bf16)
    return a, b, c


def left_parts(x):
    a, b, c = split3(x)
    return jnp.concatenate([a, a, b, a, b, c], axis=1)


def right_parts(x, axis=0):
    a, b, c = split3(x)
    return jnp.concatenate([a, b, a, c, b, a], axis=axis)


def mm(a, b):
    return jnp.dot(a, b, preferred_element_type=f32)


def mm_nt(a, b):
    return lax.dot_general(a, b, (((1,), (1,)), ((), ())), preferred_element_type=f32)


def all_rows(x, p):
    return jnp.broadcast_to(x[p : p + 1, :], x.shape)


def tree_sum(xs):
    while len(xs) > 1:
        xs = [xs[i] + xs[i + 1] if i + 1 < len(xs) else xs[i] for i in range(0, len(xs), 2)]
    return xs[0]


def sweep8(M, g):
    n = M.shape[0]
    p0 = 8 * g
    lane = lax.broadcasted_iota(jnp.int32, (8, n), 1)
    sub = lax.broadcasted_iota(jnp.int32, (8, n), 0)
    inside = (lane >= p0) & (lane < p0 + 8)
    R = M[p0 : p0 + 8, :]
    V = [jnp.broadcast_to(R[:, p0 + j : p0 + j + 1], (8, n)) for j in range(8)]
    for p in range(8):
        at = sub == p
        inv = 1.0 / all_rows(V[p], p)
        Vp = jnp.where(at, -1.0, V[p])
        V = [
            Vp * inv if j == p else jnp.where(at, 0.0, V[j]) - Vp * (all_rows(V[j], p) * inv)
            for j in range(8)
        ]
    Rq = jnp.where(inside, jnp.where(lane - p0 == sub, 1.0, 0.0), -R)
    W = tree_sum([V[r] * all_rows(Rq, r) for r in range(8)])
    Wb = [all_rows(W, r) for r in range(8)]
    out = []
    for i in range(n // 8):
        if i == g:
            out.append(W)
            continue
        Mi = M[8 * i : 8 * i + 8, :]
        t = [jnp.broadcast_to(Mi[:, p0 + r : p0 + r + 1], (8, n)) * Wb[r] for r in range(8)]
        out.append(jnp.where(inside, 0.0, Mi) - tree_sum(t))
    return jnp.concatenate(out, axis=0)


def sweep_tile(M):
    for g in range(M.shape[0] // 8):
        M = sweep8(M, g)
    return M


def halves(rows):
    tiles = [(i, j) for i in rows for j in range(i + 1)]
    cut = (len(tiles) + 1) // 2
    return tiles[:cut], tiles[cut:] + tiles[-1:] * (2 * cut - len(tiles))


def chunked(total, count):
    return tuple((total + count - 1 - c) // count for c in range(count))


def tile_at(t):
    return slice(t * TILE, (t + 1) * TILE)


def mask_kernel(counts_ref, x_ref, lead_ref, rest_ref):
    x = x_ref[...]
    live = lax.broadcasted_iota(jnp.int32, x.shape, 0) < counts_ref[lax.axis_index("dp")]
    x = jnp.where(live, x, jnp.zeros_like(x))
    cut = lead_ref.shape[1]
    lead_ref[...] = x[:, :cut]
    rest_ref[...] = x[:, cut:]


def terms_kernel(rows, parts, chunks, *refs):
    lead, refs = refs[:parts], refs[parts:]
    if rows[0] > 0:
        rest, refs = refs[:parts], refs[parts:]
    sends, refs = refs[: len(chunks)], refs[len(chunks) :]
    keep, X, XT, buf = refs
    at = 0
    cut = lead[0].shape[1]
    for p in range(parts):
        h = lead[p].shape[0]
        here = slice(at, at + h)
        X[here, :cut] = lead[p][...]
        if rows[0] > 0:
            X[here, cut:] = rest[p][...]
            XT[:, here] = rest[p][...].T
        else:
            XT[:, here] = lead[p][...].T
        at += h
    first, second = halves(rows)
    half = len(first)
    order = first + second
    for i in rows:
        r = i - rows[0]
        panel = mm(XT[tile_at(r), :], X[:, : (i + 1) * TILE])
        for t, (a, j) in enumerate(order):
            if a == i:
                buf[tile_at(t), :] = panel[:, tile_at(j)]
    low = lax.axis_index("dp") % 2 == 0
    at = 0
    for send in sends:
        for t in range(send.shape[0] // TILE):
            a, b = buf[tile_at(at), :], buf[tile_at(half + at), :]
            send[tile_at(t), :] = jnp.where(low, a, b)
            keep[tile_at(at), :] = jnp.where(low, b, a)
            at += 1


def packed_kernel(x_ref, out_ref):
    x = x_ref[...]
    xt = x.T
    at = 0
    for i in range(x.shape[1] // TILE):
        panel = mm(xt[tile_at(i), :], x[:, : (i + 1) * TILE])
        for j in range(i + 1):
            out_ref[tile_at(at), :] = panel[:, tile_at(j)]
            at += 1


def summed_tiles(rows, chunks, refs):
    if chunks is None:
        (packed,) = refs
        return (lambda i, j: packed[tile_at(i * (i + 1) // 2 + j), :]), lambda: None
    count = len(chunks)
    sends, near, far, near_other, far_other = (refs[count * q : count * (q + 1)] for q in range(5))
    keep, got, sems = refs[5 * count :]
    first, second = halves(rows)
    half = len(first)
    line = lax.axis_index("dp") // 2
    middle = (line == 1) | (line == 2)
    waits = []
    at = 0
    for q, (inner, outer) in enumerate(((near, far), (near_other, far_other))):
        for c in range(count):
            size = chunks[c] * TILE
            to = got.at[pl.ds(at, size), :]
            at += size
            sem = sems.at[q * count + c]

            @pl.when(middle)
            def _(src=inner[c], to=to, sem=sem):
                pltpu.make_async_copy(src, to, sem).start()

            @pl.when(jnp.logical_not(middle))
            def _(src=outer[c], to=to, sem=sem):
                pltpu.make_async_copy(src, to, sem).start()

            waits.append(pltpu.make_async_copy(inner[c], to, sem))
    where = [(c, t) for c in range(count) for t in range(chunks[c])]
    low = lax.axis_index("dp") % 2 == 0

    def tile(i, j):
        side = 0 if (i, j) in first else 1
        t = (second if side else first).index((i, j))
        c, u = where[t]
        mine = sends[c][tile_at(u), :] + got[tile_at(t), :]
        other = keep[tile_at(t), :] + got[tile_at(half + t), :]
        return jnp.where(low, other, mine) if side else jnp.where(low, mine, other)

    def arrive():
        for w in waits:
            w.wait()

    return tile, arrive


def damped_tile(tile, i, j, scale):
    t = tile(i, j) * scale
    if i == j:
        row = lax.broadcasted_iota(jnp.int32, (TILE, TILE), 0)
        column = lax.broadcasted_iota(jnp.int32, (TILE, TILE), 1)
        t = t + jnp.where(row == column, damping_term, 0.0)
    return t


def lead_kernel(chunks, scale_ref, *refs):
    count = 1 if chunks is None else 5 * len(chunks) + 1
    sources, (A, N), sources2 = refs[:count], refs[count : count + 2], refs[count + 2 :]
    tile, arrive = summed_tiles(range(LEAD), chunks, sources + sources2)
    arrive()
    scale = scale_ref[0]
    for i in range(LEAD):
        for j in range(i + 1):
            t = damped_tile(tile, i, j, scale)
            A[tile_at(i), tile_at(j)] = t
            if i == 0:
                N[...] = sweep_tile(t)
            if i != j:
                A[tile_at(j), tile_at(i)] = t.T


def step_kernel(k, last, a_ref, n_ref, *refs):
    if last:
        A, Cs, Ws, Wf = refs
        sweep(A, n_ref, None, tile_at(k), None, Cs, Ws, Wf)
    else:
        A, N, Cs, Ws, Wf = refs
        sweep(A, n_ref, N, tile_at(k), tile_at(k + 1), Cs, Ws, Wf)


def sweep(A, D_ref, N, here, later, Cs, Ws, Wf):
    m = A.shape[0]
    D = D_ref[...]
    Nl = left_parts(D)
    Nr = right_parts(D)
    if later is not None:
        Wn = mm(Nl, right_parts(A[here, later]))
        T = A[later, later] + mm(left_parts(A[later, here]), right_parts(Wn))
        N[...] = sweep_tile(T)
    wide = 2 * TILE
    for c in range(0, m, wide):
        w = min(wide, m - c)
        Wc = mm(Nl, right_parts(A[here, c : c + w]))
        Wf[:, c : c + w] = Wc
        Ws[:, c : c + w] = right_parts(Wc)
    for r in range(0, m, wide):
        h = min(wide, m - r)
        Cs[r : r + h, :] = left_parts(A[r : r + h, here])
    for c in range(0, m, wide):
        w = min(wide, m - c)
        A[:, c : c + w] = A[:, c : c + w] + mm(Cs[...], Ws[:, c : c + w])
    A[:, here] = -mm(Cs[...], Nr)
    A[here, :] = -Wf[...]
    A[here, here] = D


def mm6(x, y, dot):
    pairs = ((0, 2), (1, 1), (2, 0), (0, 1), (1, 0), (0, 0))
    return functools.reduce(lambda s, t: s + t, [dot(x[i], y[j]) for i, j in pairs])


def merge_kernel(chunks, own_rows, scale_ref, keep_ref, lead_ref, *refs):
    count = 1 if chunks is None else 5 * len(chunks) + 1
    sources, refs = refs[:count], refs[count:]
    if own_rows:
        grad_ref, inv_ref, kept_ref, left_ref, *refs = refs
    else:
        inv_ref, kept_ref, *refs = refs
    A, N, Qs, Ps, Cs, Ws, Wf, kept = refs[:8]
    *more, sems = refs[8:]
    n = A.shape[0]
    m = LEAD * TILE
    blocks = n // TILE
    if chunks is not None:
        more.append(sems.at[pl.ds(4, 2 * len(chunks))])
    tile, arrive = summed_tiles(range(LEAD, blocks), chunks, sources + tuple(more))
    scale = scale_ref[0]
    for c in range(0, m, 2 * TILE):
        w = min(2 * TILE, m - c)
        lead = lead_ref[:, c : c + w]
        A[:m, c : c + w] = lead
        for q, part in enumerate(split3(lead)):
            Ps[q, :, c : c + w] = part
    arrive()
    for some in (range(LEAD, LEAD + 1), range(LEAD + 1, blocks)):
        for i in some:
            for j in range(LEAD):
                for q, part in enumerate(split3(damped_tile(tile, i, j, scale))):
                    Qs[q, tile_at(i - LEAD), tile_at(j)] = part
        rows = slice((some[0] - LEAD) * TILE, (some[-1] + 1 - LEAD) * TILE)
        lower = slice(some[0] * TILE, (some[-1] + 1) * TILE)
        for c in range(0, m, 2 * TILE):
            d = slice(c, min(c + 2 * TILE, m))
            A[lower, d] = -mm6([Qs[q, rows, :] for q in range(3)], [Ps[q, :, d] for q in range(3)], mm)
        W3 = split3(A[lower, :m])
        width = (some[-1] + 1 - LEAD) * TILE
        S = mm6(W3, [Qs[q, :width, :] for q in range(3)], mm_nt)
        for i in some:
            r = tile_at(i - some[0])
            for j in range(LEAD, i + 1):
                t = damped_tile(tile, i, j, scale) - S[r, tile_at(j - LEAD)]
                A[tile_at(i), tile_at(j)] = t
                if i == LEAD:
                    N[...] = sweep_tile(t)
                if i != j:
                    A[tile_at(j), tile_at(i)] = t.T
            for j in range(LEAD):
                A[tile_at(j), tile_at(i)] = A[tile_at(i), tile_at(j)].T

    def step(k, _):
        here = pl.ds(pl.multiple_of(k * TILE, TILE), TILE)
        later = pl.ds(pl.multiple_of((k + 1) * TILE, TILE), TILE)
        sweep(A, N, N, here, later, Cs, Ws, Wf)
        return 0

    lax.fori_loop(LEAD, blocks - 1, step, 0)
    here = tile_at(blocks - 1)
    D = N[...]
    Nl = left_parts(D)
    Nr = right_parts(D)
    keep = keep_ref[0] != 0
    wide = 2 * TILE
    for c in range(0, n, wide):
        w = min(wide, n - c)
        Wc = mm(Nl, right_parts(A[here, c : c + w]))
        Wf[:, c : c + w] = Wc
        Ws[:, c : c + w] = right_parts(Wc)
    tall = n // 4
    copies = []
    for q in range(4):
        rows = slice(q * tall, (q + 1) * tall)
        C = left_parts(A[rows, here])
        for c in range(0, n - TILE, wide):
            w = min(wide, n - TILE - c)
            r = -(A[rows, c : c + w] + mm(C, Ws[:, c : c + w]))
            inv_ref[rows, c : c + w] = r.astype(bf16)
        inv_ref[rows, here] = mm(C, Nr).astype(bf16)
        if q == 3:
            inv_ref[here, :] = Wf[...].astype(bf16)
            inv_ref[here, here] = (-D).astype(bf16)
        r = inv_ref[rows, :]
        kept[rows, :] = jnp.where(keep, r, jnp.zeros_like(r))
        copy = pltpu.make_async_copy(kept.at[rows, :], kept_ref.at[rows, :], sems.at[q])
        copy.start()
        copies.append(copy)
    if own_rows:
        at = pl.multiple_of(lax.axis_index("dp") * own_rows, 16)
        left_ref[...] = mm(inv_ref[pl.ds(at, own_rows), :], grad_ref[...])
    for copy in copies:
        copy.wait()


def finish_kernel(left_ref, inv_ref, out_ref):
    left = left_ref[...]
    high = left.astype(bf16)
    low = (left - high.astype(f32)).astype(bf16)
    both = mm(jnp.concatenate([high, low], axis=0), inv_ref[...])
    rows = left.shape[0]
    out_ref[...] = (both[:rows] + both[rows:]).astype(bf16)


vmem = lambda: pl.BlockSpec(memory_space=pltpu.VMEM)
smem = lambda: pl.BlockSpec(memory_space=pltpu.SMEM)


def call(kernel, name, scalars, arrays, outs, scratch=(), aliases=None, us=5, limit=36, anys=(), any_outs=(), sems=0):
    anywhere = pl.BlockSpec(memory_space=pl.ANY)
    out = pl.pallas_call(
        kernel,
        out_shape=[jax.ShapeDtypeStruct(*o) for o in outs],
        in_specs=[smem()] * len(scalars) + [anywhere if a in anys else vmem() for a in range(len(arrays))],
        out_specs=[anywhere if a in any_outs else vmem() for a in range(len(outs))],
        scratch_shapes=[pltpu.VMEM(s, d) for s, d in scratch]
        + ([pltpu.SemaphoreType.DMA((sems,))] if sems else []),
        input_output_aliases={len(scalars) + a: b for a, b in (aliases or {}).items()},
        compiler_params=pltpu.CompilerParams(vmem_limit_bytes=limit << 20),
        cost_estimate=pl.CostEstimate(flops=int(us * 1.1e9), bytes_accessed=0, transcendentals=0),
        name=name,
    )(*scalars, *arrays)
    return out


def panel_scratch(m):
    return [((m, 6 * TILE), bf16), ((6 * TILE, m), bf16), ((TILE, m), f32)]


def sweep_step(A, N, k):
    m = A.shape[0]
    last = (k + 1) * TILE == m
    out = call(
        functools.partial(step_kernel, k, last),
        "sweep_%d" % k,
        [],
        [A, N],
        [((m, m), f32)] + ([] if last else [((TILE, TILE), f32)]),
        panel_scratch(m),
        {0: 0} if last else {0: 0, 1: 1},
        us=5,
        limit=16,
    )
    return (out[0], None) if last else out


Z_PAIR = [(2 * z + y, 2 * (z ^ 1) + y) for z in range(4) for y in range(2)]
Y_PAIR = [(i, i ^ 1) for i in range(8)]


def neighbours(x):
    return hop(x, Y_PAIR), hop(x, Z_PAIR)


def corner(across, along):
    rows = across.shape[0] // 2
    return hop(across[:rows], Z_PAIR), hop(along[rows:], Y_PAIR)


MIDDLE = [(2 * z + y, 2 * (3 - z) + y) for z in (1, 2) for y in range(2)]
OUTWARD = [(2 * a + y, 2 * b + y) for a, b in ((1, 0), (2, 3)) for y in range(2)]
SWAP_MIDDLE = [(2 * z + y, 2 * z + 1 - y) for z in (1, 2) for y in range(2)]
SWAP_END = [(2 * z + y, 2 * z + 1 - y) for z in (0, 3) for y in range(2)]


def hop(x, pairs):
    return lax.ppermute(x, "dp", pairs)


def terms(rows, parts, chunks, name):
    lead, rest = parts
    tokens = sum(p.shape[0] for p in lead)
    count = sum(chunks)
    width = (rows[-1] + 1) * TILE
    out = call(
        functools.partial(terms_kernel, rows, len(lead), chunks),
        name,
        [],
        lead + rest,
        [((c * TILE, TILE), f32) for c in chunks] + [((count * TILE, TILE), f32)],
        [
            ((tokens, width), bf16),
            ((len(rows) * TILE, tokens), bf16),
            ((2 * count * TILE, TILE), f32),
        ],
        us=4,
    )
    return out[:-1], out[-1]


def tie(*xs):
    return lax.optimization_barrier(xs)


def on_device(inputs, grad_weight, counts, owners):
    samples = inputs[0]
    n = samples.shape[1]
    blocks = n // TILE
    m = LEAD * TILE
    w = n - m
    chip = lax.axis_index("dp")
    core = lax.axis_index("owner")
    tok = samples.shape[0]
    lead, rest = call(
        mask_kernel, "mask_tokens", [counts], [samples], [((tok, m), bf16), ((tok, w), bf16)], us=1
    )
    scale = (1.0 / jnp.sum(counts).astype(f32))[None]
    keep = (owners[core] == chip).astype(jnp.int32)[None]
    dma = lambda k, at: dict(anys=range(at + k, at + 5 * k), sems=2 * k)
    if lax.axis_size("dp") == 8:
        lead_chunks = chunked(len(halves(range(LEAD))[0]), 2)
        rest_chunks = chunked(len(halves(range(LEAD, blocks))[0]), 3)
        across, along = neighbours(lead)
        leads = [lead, across, along, *corner(across, along)]
        rest = tie(rest, leads[3], leads[4])[0]
        lead_sends, lead_keep = terms(range(LEAD), (leads, []), lead_chunks, "lead_terms")
        near = [hop(x, MIDDLE) for x in lead_sends]
        across, along = neighbours(rest)
        far = [hop(x, OUTWARD) for x in near]
        near_other = [hop(x, SWAP_MIDDLE) for x in near]
        across, along, near[1], far[0] = tie(across, along, near[1], far[0])
        far_other = [hop(x, SWAP_END) for x in far]
        *diagonal, far[1] = tie(*corner(across, along), far[1])
        lead_got = near, far, near_other, far_other
        rest_sends, rest_keep = terms(
            range(LEAD, blocks), (leads, [rest, across, along, *diagonal]), rest_chunks, "rest_terms"
        )
        near = [hop(x, MIDDLE) for x in rest_sends]
        lead_src = list(lead_sends) + sum(lead_got, []) + [lead_keep]
        lead_dma = dma(len(lead_chunks), 0)
        rest_dma = dma(len(rest_chunks), 1)
        rest_dma["sems"] += 4
        lead_buf = [((2 * sum(lead_chunks) * TILE, TILE), f32)]
        rest_buf = [((2 * sum(rest_chunks) * TILE, TILE), f32)]
    else:
        lead_chunks = rest_chunks = None
        lead_dma, rest_dma = {}, dict(sems=4)
        lead_buf = rest_buf = []
        whole = jnp.concatenate([lead, rest], axis=1)
        tiles = blocks * (blocks + 1) // 2
        packed = call(packed_kernel, "own_terms", [], [whole], [((tiles * TILE, TILE), f32)])[0]
        shares = lax.psum_scatter(packed, "dp", scatter_dimension=0, tiled=True)
        lead_src = rest_src = [lax.all_gather(shares, "dp", axis=0, tiled=True)]
    A, N = call(
        functools.partial(lead_kernel, lead_chunks),
        "lead_tiles",
        [scale],
        lead_src,
        [((m, m), f32), ((TILE, TILE), f32)],
        lead_buf,
        us=0.05,
        limit=16,
        **lead_dma,
    )
    passes = {} if rest_chunks is None else {-1: 0, 1: 1, 2: 2}
    swaps = {} if rest_chunks is None else {1: 0, 3: 1, 4: 2}
    far, near_other, far_other = {}, {}, {}
    for k in range(-1, LEAD):
        if k >= 0:
            A, N = sweep_step(A, N, k)
        if k in passes:
            c = passes[k]
            N, near[c] = tie(N, near[c])
            far[c] = hop(near[c], OUTWARD)
            near_other[c] = hop(near[c], SWAP_MIDDLE)
        if k in swaps:
            c = swaps[k]
            N, far[c] = tie(N, far[c])
            far_other[c] = hop(far[c], SWAP_END)
    if rest_chunks is not None:
        count = range(len(rest_chunks))
        parts = [near] + [[d[c] for c in count] for d in (far, near_other, far_other)]
        rest_src = list(rest_sends) + sum(parts, []) + [rest_keep]
    tile = ((TILE, TILE), f32)
    rows = n // lax.axis_size("dp")
    fused = rows % 16 == 0
    inverse, kept, *left = call(
        functools.partial(merge_kernel, rest_chunks, rows if fused else 0),
        "rest_tiles",
        [scale, keep],
        [A] + rest_src + ([grad_weight] if fused else []),
        [((n, n), bf16)] * 2 + ([((rows, n), f32)] if fused else []),
        [((n, n), f32), tile, ((3, w, m), bf16), ((3, m, m), bf16)]
        + panel_scratch(n)
        + [((n, n), bf16)]
        + rest_buf,
        us=30,
        limit=44,
        any_outs=(1,),
        **rest_dma,
    )
    if fused:
        left = left[0]
    else:
        part = lax.dynamic_slice_in_dim(inverse, chip * rows, rows, 0)
        left = jnp.dot(part, grad_weight, preferred_element_type=f32)
    left = lax.ppermute(left, "owner", [(1, 0)])
    both = call(finish_kernel, "finish", [], [left, inverse], [((rows, n), bf16)], us=1, limit=36)[0]
    half = rows // 2
    other = lax.ppermute(both[half:], "owner", [(0, 1)])
    precond = jnp.where(core == 0, both[:half], other)
    return (kept[None, None], precond)


def solution(mesh):
    return jax.shard_map(
        on_device,
        mesh=mesh,
        in_specs=(P("owner", ("groups", "dp"), None), P("groups", None), P("groups"), P("groups")),
        out_specs=(P(("groups", "dp"), "owner", None, None), P(("groups", "dp", "owner"), None)),
        check_vma=False,
    )
```
